32 devices in a mesh: rows: 8 (over y, x, core), cols: 4 (over z).
Axes of the slice: x: 2, y: 2, z: 4, core: 2. Of those that a mesh axis runs over, the one named last changes fastest.
Arguments:
- anomalies: bfloat16 [16384, 64], P(('rows', 'cols')), may hold values from -6 to 6
- innovations: bfloat16 [16384, 64], P(('rows', 'cols')), may hold values from -3 to 3
- pair_rows: int32 [8, 2048], P('rows', 'cols'), may hold values from 0 to 15, as said below
- pair_cols: int32 [8, 2048], P('rows', 'cols'), may hold values from 0 to 31
- pair_dist: int32 [8, 2048], P('rows', 'cols'), may hold values from 0 to 7
- pair_counts: int32 [8, 4], P('rows', 'cols'), may hold values from 64 to 512, as said below
Outputs:
- increment: float32 [16384, 64], P(('rows', 'cols'))
The draws below stay inside these ranges and needn't reach their ends.
Inputs may be any that keep to these rules, and one draw needn't show every extreme that they name: In the 512 slots of one device the pairs (pair_rows, pair_cols) are distinct, and each row block stands in at most 32 of them. `pair_counts`: some device has all its slots live in every draw.
All inputs are finite; a program needn't handle non-finite values.
Results may differ from the reference program's by a relative error of at most 0.005.
Values may be sent and summed in bfloat16 or wider, within the bound.
No kernel may reach another device: no remote copies, remote signals or barrier semaphores. Data moves between devices by JAX's collectives and lax.ppermute only.
A program may use at most 128 MiB of HBM per device.

```python
import jax
import jax.numpy as jnp
from jax import lax

BLK = 128
M = 64
K = 64
TAPER_CELLS = 8
DMAX = 8
CELL_DEV = 512
PAIRS_BLOCK = 32
RBLK = 16
CBLK = 32
P_DEV = 512
NCELLS = 16384
N_ROWS = 8
N_COLS = 4


def slot_pairs(key):
    device_total = N_ROWS * N_COLS
    perm_key = jax.random.fold_in(key, 11)
    shuffle_key = jax.random.fold_in(key, 17)
    perm_keys = jax.random.split(perm_key, device_total * RBLK)
    col_perms = jax.vmap(lambda one_key: jax.random.permutation(one_key, CBLK))(perm_keys)
    chosen = col_perms[:, :PAIRS_BLOCK].reshape(device_total, P_DEV)
    row_table = jnp.repeat(jnp.arange(RBLK), PAIRS_BLOCK)
    row_table = jnp.broadcast_to(row_table[None, :], (device_total, P_DEV))
    shuffle_keys = jax.random.split(shuffle_key, device_total)
    orders = jax.vmap(lambda one_key: jax.random.permutation(one_key, P_DEV))(shuffle_keys)
    row_out = jnp.take_along_axis(row_table, orders, axis=1)
    col_out = jnp.take_along_axis(chosen, orders, axis=1)
    return (row_out.reshape(N_ROWS, N_COLS * P_DEV).astype(jnp.int32), col_out.reshape(N_ROWS, N_COLS * P_DEV).astype(jnp.int32))


def draw_pair_rows(key, part):
    return slot_pairs(key)[0]


def draw_pair_cols(key, part):
    return slot_pairs(key)[1]


def draw_pair_counts(key, part):
    base_key = jax.random.fold_in(key, 29)
    flame_key, high_key, low_key, top_key = jax.random.split(base_key, 4)
    flame = jax.random.randint(flame_key, (), 0, N_ROWS)
    row_index = jnp.arange(N_ROWS)[:, None]
    col_index = jnp.arange(N_COLS)[None, :]
    apart = jnp.abs(row_index - flame)
    cycle_apart = jnp.minimum(apart, N_ROWS - apart)
    near_flame = cycle_apart <= N_ROWS // 8
    high_load = jax.random.randint(high_key, (N_ROWS, N_COLS), P_DEV // 2, P_DEV + 1)
    low_load = jax.random.randint(low_key, (N_ROWS, N_COLS), P_DEV // 8, P_DEV // 3 + 1)
    loads = jnp.where(near_flame, high_load, low_load)
    top_col = jax.random.randint(top_key, (), 0, N_COLS)
    loads = jnp.where((row_index == flame) & (col_index == top_col), P_DEV, loads)
    return loads.astype(jnp.int32)


def touch_ends(entries, rng, low, high):
    longest = entries.shape.index(max(entries.shape))
    spots = []
    for shift in (0, 1):
        where = [jax.random.randint(jax.random.fold_in(rng, axis), (), 0, length) for axis, length in enumerate(entries.shape)]
        where[longest] = (where[longest] + shift) % entries.shape[longest]
        spots.append(tuple(where))
    return entries.at[spots[0]].set(low).at[spots[1]].set(high)


def level_of(stream_key, extent, pieces, low, high):
    factor_of, own = 1.0, jax.random.fold_in(stream_key, 6)
    for dim, blocks in pieces:
        steps = jnp.exp(jax.random.uniform(jax.random.fold_in(own, dim), (blocks,), jnp.float32, low / len(pieces), high / len(pieces)))
        factor_of = factor_of * jnp.repeat(steps, extent[dim] // blocks).reshape([-1 if axis == dim else 1 for axis in range(len(extent))])
    return factor_of


def bell_draw(key, shape, spread, bound, shards=(), kind=jnp.bfloat16):
    values = jax.random.normal(key, shape, jnp.float32) * spread
    if len(shards) > 0:
        values = level_of(key, shape, shards, -0.22, 0.18) * values
    return jnp.clip(values, min=-bound, max=bound).astype(kind)


def setup_inputs(seed: int = 0) -> dict:
    streams_of = jax.random.split(jax.random.key(seed), 7)
    return {
        "anomalies": bell_draw(streams_of[0], (NCELLS, M), 1.0, 6.0, ((0, 32),)),
        "innovations": bell_draw(streams_of[1], (NCELLS, K), 0.5, 3.0, ((0, 32),)),
        "pair_rows": draw_pair_rows(jax.random.fold_in(streams_of[6], 71), 0),
        "pair_cols": draw_pair_cols(jax.random.fold_in(streams_of[6], 71), 0),
        "pair_dist": touch_ends(jax.random.randint(streams_of[4], (N_ROWS, N_COLS * P_DEV), 0, DMAX), jax.random.fold_in(streams_of[4], 1), 0, DMAX - 1).astype(jnp.int32),
        "pair_counts": draw_pair_counts(jax.random.fold_in(streams_of[6], 71), 0),
    }


DIST_SCALE = 4.0


def reference(anomalies, innovations, pair_rows, pair_cols, pair_dist, pair_counts):
    per_dev = CELL_DEV // BLK
    anom_blocks = anomalies.reshape(NCELLS // BLK, BLK, M)
    innov_blocks = innovations.reshape(NCELLS // BLK, BLK, K)
    offsets = jnp.arange(BLK)
    kernel = jnp.exp(-jnp.abs(offsets[:, None] - offsets[None, :]).astype(jnp.float32) / TAPER_CELLS)
    row_ids = pair_rows.reshape(N_ROWS * N_COLS, P_DEV)
    col_ids = pair_cols.reshape(N_ROWS * N_COLS, P_DEV)
    distances = pair_dist.reshape(N_ROWS * N_COLS, P_DEV)
    live_counts = pair_counts.reshape(N_ROWS * N_COLS)
    slot_index = jnp.arange(P_DEV)
    block_index = jnp.arange(RBLK)

    def device_part(device):
        row_index = device // N_COLS
        col_range = device % N_COLS
        local_rows = row_ids[device]
        col_local = col_ids[device]
        first_blocks = row_index * RBLK + local_rows
        second_blocks = (col_local // per_dev) * RBLK + col_range * per_dev + col_local % per_dev
        live_slot = slot_index < live_counts[device]
        left = anom_blocks[first_blocks].astype(jnp.float32)
        right = anom_blocks[second_blocks].astype(jnp.float32)
        innov = innov_blocks[second_blocks].astype(jnp.float32)
        products = jnp.einsum('pim,pjm->pij', left, right)
        block_weight = jnp.where(live_slot, jnp.exp(-distances[device].astype(jnp.float32) / DIST_SCALE), 0.0)
        tapered = (products * (1.0 / (M - 1)) * block_weight[:, None, None] * kernel).astype(jnp.bfloat16)
        applied = jnp.einsum('pij,pjk->pik', tapered.astype(jnp.float32), innov)
        onehot = (local_rows[:, None] == block_index[None, :]).astype(jnp.float32)
        return jnp.einsum('pr,pik->rik', onehot, applied)

    partials = lax.map(device_part, jnp.arange(N_ROWS * N_COLS))
    summed = partials.reshape(N_ROWS, N_COLS, RBLK * BLK, K).sum(axis=1)
    return summed.reshape(NCELLS, K)
```

```python
import jax
import jax.numpy as jnp
from jax import lax
from jax.experimental import pallas as pl
from jax.experimental.pallas import tpu as pltpu
from jax.sharding import PartitionSpec as P

BLK = 128
TAPER_CELLS = 8
DIST_SCALE = 4.0
DMAX = 8
HALF = 256

F32 = jnp.float32
BF16 = jnp.bfloat16
VMEM = pl.BlockSpec(memory_space=pltpu.VMEM)
SMEM = pl.BlockSpec(memory_space=pltpu.SMEM)


def table_kernel(per_dev, rows_ref, cols_ref, dist_ref, count_ref, table_ref):
    slots = rows_ref.shape[1]
    row_blocks, col_blocks = table_ref.shape
    row_flip = lax.axis_index("cols") * per_dev
    col_flip = lax.axis_index("rows") * per_dev
    live = lax.broadcasted_iota(jnp.int32, (1, slots), 1) < count_ref[0, 0]
    code = jnp.where(live, dist_ref[...] + 1, 0).astype(F32)
    row_place = lax.broadcasted_iota(jnp.int32, (row_blocks, slots), 0)
    col_place = lax.broadcasted_iota(jnp.int32, (col_blocks, slots), 0)
    left = jnp.where(row_place == (rows_ref[...] ^ row_flip), code, 0.0).astype(BF16)
    right = jnp.where(col_place == (cols_ref[...] ^ col_flip), 1.0, 0.0).astype(BF16)
    table = lax.dot_general(left, right, (((1,), (1,)), ((), ())), preferred_element_type=F32)
    table_ref[...] = table.astype(jnp.int32)


def pair_table(pair_rows, pair_cols, pair_dist, pair_counts, row_blocks, col_blocks, per_dev):
    def kernel(*refs):
        table_kernel(per_dev, *refs)

    return pl.pallas_call(
        kernel,
        out_shape=jax.ShapeDtypeStruct((row_blocks, col_blocks), jnp.int32),
        in_specs=[VMEM, VMEM, VMEM, SMEM],
        out_specs=VMEM,
        name="pair_table",
    )(pair_rows, pair_cols, pair_dist, pair_counts)


def increment_rows(table, first, row_part, col_parts, out_dtype):
    members, cells = row_part.shape
    columns = col_parts[0].shape[0] - members
    blocks = cells // BLK
    halves = cells // HALF
    per_half = HALF // BLK

    def kernel(table_ref, row_ref, *refs):
        col_refs, out_ref, taper_ref = refs[:-2], refs[-2], refs[-1]
        gap = lax.broadcasted_iota(jnp.int32, (BLK, BLK), 0) - lax.broadcasted_iota(jnp.int32, (BLK, BLK), 1)
        base = jnp.exp(-jnp.abs(gap).astype(F32) / TAPER_CELLS) * (1.0 / (members - 1))
        taper_ref[0] = jnp.zeros((BLK, BLK), F32)
        for dist in range(DMAX):
            taper_ref[dist + 1] = base * jnp.exp(jnp.full((1, 1), -dist / DIST_SCALE, F32))
        left = row_ref[...].T
        total = jnp.zeros((cells, columns), F32)
        for part, col_ref in enumerate(col_refs):
            for half in range(halves):
                span = pl.ds(half * HALF, HALF)
                right = col_ref[pl.ds(0, members), span]
                innov = col_ref[pl.ds(members, columns), span]
                products = jnp.dot(left, right, preferred_element_type=F32)
                first_col = part * blocks + half * per_half
                tapered = jnp.concatenate(
                    [
                        jnp.concatenate(
                            [
                                products[a * BLK : (a + 1) * BLK, q * BLK : (q + 1) * BLK]
                                * taper_ref[table_ref[first + a, first_col + q]]
                                for q in range(per_half)
                            ],
                            axis=1,
                        ).astype(BF16)
                        for a in range(blocks)
                    ],
                    axis=0,
                )
                total = total + lax.dot_general(
                    tapered, innov, (((1,), (1,)), ((), ())), preferred_element_type=F32
                )
        out_ref[...] = total.T.astype(out_dtype)

    count = len(col_parts)
    pairs = blocks * blocks * count
    return pl.pallas_call(
        kernel,
        out_shape=jax.ShapeDtypeStruct((columns, cells), out_dtype),
        in_specs=[SMEM] + [VMEM] * (1 + count),
        out_specs=VMEM,
        scratch_shapes=[pltpu.VMEM((DMAX + 1, BLK, BLK), F32)],
        cost_estimate=pl.CostEstimate(
            flops=4 * pairs * BLK * BLK * members,
            bytes_accessed=count * (members + columns) * cells * 2,
            transcendentals=BLK * BLK,
        ),
        name="increment_rows",
    )(table, row_part, *col_parts)


def swap(x, axis, size, flip):
    return lax.ppermute(x, axis, [(i, i ^ flip) for i in range(size)])


def solution(mesh):
    n_rows, n_cols = mesh.shape["rows"], mesh.shape["cols"]

    def local(anomalies, innovations, pair_rows, pair_cols, pair_dist, pair_counts):
        per_dev = anomalies.shape[0] // BLK
        anom, innov = anomalies.T, innovations.T
        packed = jnp.concatenate([anom, innov], axis=0)
        table = pair_table(
            pair_rows, pair_cols, pair_dist, pair_counts, n_cols * per_dev, n_rows * per_dev, per_dev
        )
        col_parts = [None] * n_rows
        for flip in range(0, n_rows, 2):
            col_parts[flip] = packed if flip == 0 else swap(packed, "rows", n_rows, flip)
        for flip in range(0, n_rows, 2):
            col_parts[flip + 1] = swap(col_parts[flip], "rows", n_rows, 1)
        row_parts = [anom if flip == 0 else swap(anom, "cols", n_cols, flip) for flip in range(n_cols)]
        received = []
        for flip in range(n_cols - 1, 0, -1):
            part = increment_rows(table, flip * per_dev, row_parts[flip], col_parts, BF16)
            received.append(swap(part, "cols", n_cols, flip))
        total = increment_rows(table, 0, row_parts[0], col_parts, F32)
        for part in received:
            total = total + part.astype(F32)
        return total.T

    spread = P(("rows", "cols"), None)
    pairs = P("rows", "cols")
    return jax.shard_map(
        local,
        mesh=mesh,
        in_specs=(spread, spread, pairs, pairs, pairs, pairs),
        out_specs=spread,
        check_vma=False,
    )
```

```python
import jax
import jax.numpy as jnp
from jax import lax
from jax.experimental import pallas as pl
from jax.experimental.pallas import tpu as pltpu
from jax.sharding import PartitionSpec as P

BLK = 128
TAPER_CELLS = 8
DIST_SCALE = 4.0
DMAX = 8
HALF = 256

F32 = jnp.float32
BF16 = jnp.bfloat16
VMEM = pl.BlockSpec(memory_space=pltpu.VMEM)
SMEM = pl.BlockSpec(memory_space=pltpu.SMEM)


def pair_table(pair_rows, pair_cols, pair_dist, pair_counts, row_blocks, col_blocks, per_dev):
    def kernel(rows_ref, cols_ref, dist_ref, count_ref, table_ref):
        slots = rows_ref.shape[1]
        row_flip = lax.axis_index("cols") * per_dev
        col_flip = lax.axis_index("rows") * per_dev
        live = lax.broadcasted_iota(jnp.int32, (1, slots), 1) < count_ref[0, 0]
        code = jnp.where(live, dist_ref[...] + 1, 0).astype(F32)
        row_place = lax.broadcasted_iota(jnp.int32, (row_blocks, slots), 0)
        col_place = lax.broadcasted_iota(jnp.int32, (col_blocks, slots), 0)
        left = jnp.where(row_place == (rows_ref[...] ^ row_flip), code, 0.0).astype(BF16)
        right = jnp.where(col_place == (cols_ref[...] ^ col_flip), 1.0, 0.0).astype(BF16)
        table = lax.dot_general(left, right, (((1,), (1,)), ((), ())), preferred_element_type=F32)
        table_ref[...] = table.astype(jnp.int32)

    return pl.pallas_call(
        kernel,
        out_shape=jax.ShapeDtypeStruct((row_blocks, col_blocks), jnp.int32),
        in_specs=[VMEM, VMEM, VMEM, SMEM],
        out_specs=VMEM,
        name="pair_table",
    )(pair_rows, pair_cols, pair_dist, pair_counts)


def increment_rows(table, row_parts, col_parts, row_flips, col_flips, before, send):
    members, cells = row_parts[0].shape
    columns = col_parts[0].shape[0] - members
    blocks = cells // BLK
    halves = cells // HALF
    per_half = HALF // BLK
    n_row, n_col, n_before = len(row_parts), len(col_parts), len(before)

    def kernel(table_ref, *refs):
        refs = list(refs)
        row_refs, col_refs, before_refs, out_refs = (
            [refs.pop(0) for _ in range(n)] for n in (n_row, n_col, n_before, n_row)
        )
        taper_ref, left_ref, total_ref = refs
        gap = lax.broadcasted_iota(jnp.int32, (BLK, BLK), 0) - lax.broadcasted_iota(jnp.int32, (BLK, BLK), 1)
        base = jnp.exp(-jnp.abs(gap).astype(F32) / TAPER_CELLS) * (1.0 / (members - 1))
        weights = jnp.exp(lax.broadcasted_iota(jnp.int32, (1, BLK), 1).astype(F32) / -DIST_SCALE)
        taper_ref[0] = jnp.zeros((BLK, BLK), F32)
        for dist in range(DMAX):
            taper_ref[dist + 1] = base * weights[0:1, dist : dist + 1]
        for row in range(n_row):
            left_ref[...] = row_refs[row][...].T
            sum_ref = total_ref if send is not None else out_refs[row]
            for col in range(n_col):
                total = None
                for half in range(halves):
                    span = pl.ds(half * HALF, HALF)
                    right = col_refs[col][pl.ds(0, members), span]
                    innov = col_refs[col][pl.ds(members, columns), span]
                    products = jnp.dot(left_ref[...], right, preferred_element_type=F32)
                    first_row = row_flips[row] * blocks
                    first_col = col_flips[col] * blocks + half * per_half
                    tapered = jnp.concatenate(
                        [
                            jnp.concatenate(
                                [
                                    products[a * BLK : (a + 1) * BLK, q * BLK : (q + 1) * BLK]
                                    * taper_ref[table_ref[first_row + a, first_col + q]]
                                    for q in range(per_half)
                                ],
                                axis=1,
                            ).astype(BF16)
                            for a in range(blocks)
                        ],
                        axis=0,
                    )
                    applied = lax.dot_general(
                        tapered, innov, (((1,), (1,)), ((), ())), preferred_element_type=F32
                    )
                    total = applied if total is None else total + applied
                if col > 0:
                    total = total + sum_ref[...]
                elif n_before > 0:
                    total = total + before_refs[row][...]
                sum_ref[...] = total
            if send is not None:
                out_refs[row][...] = sum_ref[...].astype(send).T

    pairs = blocks * blocks * n_row * n_col
    out = (cells, columns) if send is None else (columns, cells)
    return pl.pallas_call(
        kernel,
        out_shape=[jax.ShapeDtypeStruct(out, F32 if send is None else send)] * n_row,
        in_specs=[SMEM] + [VMEM] * (n_row + n_col + n_before),
        out_specs=[VMEM] * n_row,
        scratch_shapes=[
            pltpu.VMEM((DMAX + 1, BLK, BLK), F32),
            pltpu.VMEM((cells, members), BF16),
            pltpu.VMEM((cells, columns), F32),
        ],
        compiler_params=pltpu.CompilerParams(vmem_limit_bytes=24 * 2**20),
        cost_estimate=pl.CostEstimate(
            flops=16 * pairs * BLK * BLK * members,
            bytes_accessed=n_col * (members + columns) * cells * 2,
            transcendentals=BLK * BLK,
        ),
        name="increment_rows",
    )(table, *row_parts, *col_parts, *before)


def add_up(own, received):
    def kernel(*refs):
        total = refs[0][...]
        for ref in refs[1:-1]:
            total = total + ref[...].astype(F32)
        refs[-1][...] = total

    return pl.pallas_call(
        kernel,
        out_shape=jax.ShapeDtypeStruct(own.shape, F32),
        in_specs=[VMEM] * (1 + len(received)),
        out_specs=VMEM,
        name="add_up",
    )(own, *received)


def swap(x, axis, size, flip):
    return lax.ppermute(x, axis, [(i, i ^ flip) for i in range(size)])


def solution(mesh):
    n_rows, n_cols = mesh.shape["rows"], mesh.shape["cols"]

    def local(anomalies, innovations, pair_rows, pair_cols, pair_dist, pair_counts):
        per_dev = anomalies.shape[0] // BLK
        anom, innov = anomalies.T, innovations.T
        packed = jnp.concatenate([anom, innov], axis=0)
        near = list(range(0, n_rows, 2))
        far = [flip + 1 for flip in near]
        near_parts = [packed] + [swap(packed, "rows", n_rows, flip) for flip in near[1:]]
        others = list(range(n_cols - 1, 0, -1))
        row_parts = [swap(anom, "cols", n_cols, flip) for flip in others]
        table = pair_table(
            pair_rows, pair_cols, pair_dist, pair_counts, n_cols * per_dev, n_rows * per_dev, per_dev
        )
        *near_parts, table = lax.optimization_barrier((*near_parts, *row_parts, table))
        near_parts, row_parts = near_parts[: len(near)], near_parts[len(near) :]
        far_parts = [swap(part, "rows", n_rows, 1) for part in near_parts]
        before = increment_rows(table, row_parts, near_parts, others, near, [], None)
        received = []
        for i, flip in enumerate(others):
            (part,) = increment_rows(table, [row_parts[i]], far_parts, [flip], far, [before[i]], BF16)
            received.append(swap(part, "cols", n_cols, flip))
        (own,) = increment_rows(table, [anom], near_parts + far_parts, [0], near + far, [], F32)
        return add_up(own, received).T

    spread = P(("rows", "cols"), None)
    pairs = P("rows", "cols")
    return jax.shard_map(
        local,
        mesh=mesh,
        in_specs=(spread, spread, pairs, pairs, pairs, pairs),
        out_specs=spread,
        check_vma=False,
    )
```

```python
import jax
import jax.numpy as jnp
from jax import lax
from jax.experimental import pallas as pl
from jax.experimental.pallas import tpu as pltpu
from jax.sharding import PartitionSpec as P

BLK = 128
TAPER_CELLS = 8
DIST_SCALE = 4.0
DMAX = 8
HALF = 256
SMALL = pltpu.CompilerParams(vmem_limit_bytes=4 * 2**20)

F32 = jnp.float32
BF16 = jnp.bfloat16
VMEM = pl.BlockSpec(memory_space=pltpu.VMEM)
SMEM = pl.BlockSpec(memory_space=pltpu.SMEM)


def pair_table(pair_rows, pair_cols, pair_dist, pair_counts, row_blocks, col_blocks, per_dev, members):
    def kernel(rows_ref, cols_ref, dist_ref, count_ref, table_ref):
        slots = rows_ref.shape[1]
        row_flip = lax.axis_index("cols") * per_dev
        col_flip = lax.axis_index("rows") * per_dev
        live = lax.broadcasted_iota(jnp.int32, (1, slots), 1) < count_ref[0, 0]
        code = jnp.where(live, dist_ref[...] + 1, 0).astype(F32)
        row_place = lax.broadcasted_iota(jnp.int32, (row_blocks, slots), 0)
        col_place = lax.broadcasted_iota(jnp.int32, (col_blocks, slots), 0)
        left = jnp.where(row_place == (rows_ref[...] ^ row_flip), code, 0.0).astype(BF16)
        right = jnp.where(col_place == (cols_ref[...] ^ col_flip), 1.0, 0.0).astype(BF16)
        table = lax.dot_general(left, right, (((1,), (1,)), ((), ())), preferred_element_type=F32)
        spread = lax.broadcasted_iota(jnp.int32, (col_blocks, col_blocks * BLK), 1) // BLK
        spread = (spread == lax.broadcasted_iota(jnp.int32, spread.shape, 0)).astype(F32).astype(BF16)
        wide = jnp.dot(table.astype(BF16), spread, preferred_element_type=F32)
        weight = jnp.exp((1.0 - wide) / DIST_SCALE) * (1.0 / (members - 1))
        table_ref[...] = jnp.where(wide > 0.5, weight, 0.0)

    return pl.pallas_call(
        kernel,
        out_shape=jax.ShapeDtypeStruct((row_blocks, col_blocks * BLK), F32),
        in_specs=[VMEM, VMEM, VMEM, SMEM],
        out_specs=VMEM,
        compiler_params=SMALL,
        name="pair_table",
    )(pair_rows, pair_cols, pair_dist, pair_counts)


def increment_rows(table, row_parts, col_parts, row_flips, col_flips, before, send):
    members, cells = row_parts[0].shape
    columns = col_parts[0].shape[0] - members
    blocks = cells // BLK
    halves = cells // HALF
    per_half = HALF // BLK
    n_row, n_col, n_before = len(row_parts), len(col_parts), len(before)

    def kernel(table_ref, *refs):
        refs = list(refs)
        row_refs, col_refs, before_refs, out_refs = (
            [refs.pop(0) for _ in range(n)] for n in (n_row, n_col, n_before, n_row)
        )
        taper_ref, left_ref, total_ref = refs
        gap = lax.broadcasted_iota(jnp.int32, (BLK, BLK), 0) - lax.broadcasted_iota(jnp.int32, (BLK, BLK), 1)
        taper_ref[...] = jnp.exp(-jnp.abs(gap).astype(F32) / TAPER_CELLS)
        for row in range(n_row):
            left_ref[...] = row_refs[row][...].T
            sum_ref = total_ref if send is not None else out_refs[row]
            for col in range(n_col):
                total = None
                for half in range(halves):
                    span = pl.ds(half * HALF, HALF)
                    right = col_refs[col][pl.ds(0, members), span]
                    innov = col_refs[col][pl.ds(members, columns), span]
                    products = jnp.dot(left_ref[...], right, preferred_element_type=F32)
                    first_row = row_flips[row] * blocks
                    first_col = col_flips[col] * blocks + half * per_half
                    tapered = jnp.concatenate(
                        [
                            jnp.concatenate(
                                [
                                    products[a * BLK : (a + 1) * BLK, q * BLK : (q + 1) * BLK]
                                    * (taper_ref[...] * table_ref[pl.ds(first_row + a, 1), pl.ds((first_col + q) * BLK, BLK)])
                                    for q in range(per_half)
                                ],
                                axis=1,
                            ).astype(BF16)
                            for a in range(blocks)
                        ],
                        axis=0,
                    )
                    applied = lax.dot_general(
                        tapered, innov, (((1,), (1,)), ((), ())), preferred_element_type=F32
                    )
                    total = applied if total is None else total + applied
                if col > 0:
                    total = total + sum_ref[...]
                elif n_before > 0:
                    total = total + before_refs[row][...]
                sum_ref[...] = total
            if send is not None:
                out_refs[row][...] = sum_ref[...].astype(send).T

    pairs = blocks * blocks * n_row * n_col
    out = (cells, columns) if send is None else (columns, cells)
    return pl.pallas_call(
        kernel,
        out_shape=[jax.ShapeDtypeStruct(out, F32 if send is None else send)] * n_row,
        in_specs=[VMEM] + [VMEM] * (n_row + n_col + n_before),
        out_specs=[VMEM] * n_row,
        scratch_shapes=[
            pltpu.VMEM((BLK, BLK), F32),
            pltpu.VMEM((cells, members), BF16),
            pltpu.VMEM((cells, columns), F32),
        ],
        compiler_params=pltpu.CompilerParams(vmem_limit_bytes=24 * 2**20),
        cost_estimate=pl.CostEstimate(
            flops=16 * pairs * BLK * BLK * members,
            bytes_accessed=n_col * (members + columns) * cells * 2,
            transcendentals=BLK * BLK,
        ),
        name="increment_rows",
    )(table, *row_parts, *col_parts, *before)


def add_up(own, received):
    def kernel(*refs):
        total = refs[0][...]
        for ref in refs[1:-1]:
            total = total + ref[...].astype(F32)
        refs[-1][...] = total

    return pl.pallas_call(
        kernel,
        out_shape=jax.ShapeDtypeStruct(own.shape, F32),
        in_specs=[VMEM] * (1 + len(received)),
        out_specs=VMEM,
        compiler_params=SMALL,
        name="add_up",
    )(own, *received)


def swap(x, axis, size, flip):
    return lax.ppermute(x, axis, [(i, i ^ flip) for i in range(size)])


def solution(mesh):
    n_rows, n_cols = mesh.shape["rows"], mesh.shape["cols"]

    def local(anomalies, innovations, pair_rows, pair_cols, pair_dist, pair_counts):
        per_dev = anomalies.shape[0] // BLK
        anom, innov = anomalies.T, innovations.T
        packed = jnp.concatenate([anom, innov], axis=0)
        near = list(range(0, n_rows, 2))
        far = [flip + 1 for flip in near]
        near_parts = [packed] + [swap(packed, "rows", n_rows, flip) for flip in near[1:]]
        others = list(range(n_cols - 1, 0, -1))
        row_parts = [swap(anom, "cols", n_cols, flip) for flip in others]
        table = pair_table(
            pair_rows, pair_cols, pair_dist, pair_counts, n_cols * per_dev, n_rows * per_dev, per_dev, anomalies.shape[1]
        )
        *near_parts, table = lax.optimization_barrier((*near_parts, *row_parts, table))
        near_parts, row_parts = near_parts[: len(near)], near_parts[len(near) :]
        far_parts = [swap(part, "rows", n_rows, 1) for part in near_parts]
        before = increment_rows(table, row_parts, near_parts, others, near, [], None)
        received = []
        for group in [[i] for i in range(len(others))]:
            parts = increment_rows(
                table,
                [row_parts[i] for i in group],
                far_parts,
                [others[i] for i in group],
                far,
                [before[i] for i in group],
                BF16,
            )
            received += [swap(part, "cols", n_cols, others[i]) for i, part in zip(group, parts)]
        (own,) = increment_rows(table, [anom], near_parts + far_parts, [0], near + far, [], F32)
        return add_up(own, received).T

    spread = P(("rows", "cols"), None)
    pairs = P("rows", "cols")
    return jax.shard_map(
        local,
        mesh=mesh,
        in_specs=(spread, spread, pairs, pairs, pairs, pairs),
        out_specs=spread,
        check_vma=False,
    )
```

```python
import jax
import jax.numpy as jnp
from jax import lax
from jax.experimental import pallas as pl
from jax.experimental.pallas import tpu as pltpu
from jax.sharding import PartitionSpec as P

BLK = 128
TAPER_CELLS = 8
DIST_SCALE = 4.0
DMAX = 8
HALF = 256
SMALL = pltpu.CompilerParams(vmem_limit_bytes=4 * 2**20)

F32 = jnp.float32
BF16 = jnp.bfloat16
VMEM = pl.BlockSpec(memory_space=pltpu.VMEM)
SMEM = pl.BlockSpec(memory_space=pltpu.SMEM)


def pair_table(pair_rows, pair_cols, pair_dist, pair_counts, row_blocks, col_blocks, per_dev, members):
    def kernel(rows_ref, cols_ref, dist_ref, count_ref, table_ref):
        slots = rows_ref.shape[1]
        row_flip = lax.axis_index("cols") * per_dev
        col_flip = lax.axis_index("rows") * per_dev
        live = lax.broadcasted_iota(jnp.int32, (1, slots), 1) < count_ref[0, 0]
        code = jnp.where(live, dist_ref[...] + 1, 0).astype(F32)
        row_place = lax.broadcasted_iota(jnp.int32, (row_blocks, slots), 0)
        col_place = lax.broadcasted_iota(jnp.int32, (col_blocks, slots), 0)
        left = jnp.where(row_place == (rows_ref[...] ^ row_flip), code, 0.0).astype(BF16)
        right = jnp.where(col_place == (cols_ref[...] ^ col_flip), 1.0, 0.0).astype(BF16)
        table = lax.dot_general(left, right, (((1,), (1,)), ((), ())), preferred_element_type=F32)
        spread = lax.broadcasted_iota(jnp.int32, (col_blocks, col_blocks * BLK), 1) // BLK
        spread = (spread == lax.broadcasted_iota(jnp.int32, spread.shape, 0)).astype(F32).astype(BF16)
        wide = jnp.dot(table.astype(BF16), spread, preferred_element_type=F32)
        weight = jnp.exp((1.0 - wide) / DIST_SCALE) * (1.0 / (members - 1))
        table_ref[...] = jnp.where(wide > 0.5, weight, 0.0)

    return pl.pallas_call(
        kernel,
        out_shape=jax.ShapeDtypeStruct((row_blocks, col_blocks * BLK), F32),
        in_specs=[VMEM, VMEM, VMEM, SMEM],
        out_specs=VMEM,
        compiler_params=SMALL,
        name="pair_table",
    )(pair_rows, pair_cols, pair_dist, pair_counts)


def increment_rows(table, places, row_flips, members, col_parts, col_flips, before, send):
    cells = col_parts[0].shape[1]
    columns = col_parts[0].shape[0] - members
    blocks = cells // BLK
    halves = cells // HALF
    per_half = HALF // BLK
    row_stacks = []
    for stacked, _ in places:
        if all(stacked is not known for known in row_stacks):
            row_stacks.append(stacked)
    spots = [
        ([stacked is known for known in row_stacks].index(True), start) for stacked, start in places
    ]
    n_row, n_stack, n_col, n_before = len(places), len(row_stacks), len(col_parts), len(before)

    def kernel(table_ref, *refs):
        refs = list(refs)
        row_refs, col_refs, before_refs, out_refs = (
            [refs.pop(0) for _ in range(n)] for n in (n_stack, n_col, n_before, n_row)
        )
        taper_ref, left_ref, total_ref = refs
        gap = lax.broadcasted_iota(jnp.int32, (BLK, BLK), 0) - lax.broadcasted_iota(jnp.int32, (BLK, BLK), 1)
        taper_ref[...] = jnp.exp(-jnp.abs(gap).astype(F32) / TAPER_CELLS)
        for row in range(n_row):
            left_ref[...] = row_refs[spots[row][0]][pl.ds(spots[row][1], members), :].T
            sum_ref = total_ref if send is not None else out_refs[row]
            for col in range(n_col):
                total = None
                for half in range(halves):
                    span = pl.ds(half * HALF, HALF)
                    right = col_refs[col][pl.ds(0, members), span]
                    innov = col_refs[col][pl.ds(members, columns), span]
                    products = jnp.dot(left_ref[...], right, preferred_element_type=F32)
                    first_row = row_flips[row] * blocks
                    first_col = col_flips[col] * blocks + half * per_half
                    tapered = jnp.concatenate(
                        [
                            jnp.concatenate(
                                [
                                    products[a * BLK : (a + 1) * BLK, q * BLK : (q + 1) * BLK]
                                    * (taper_ref[...] * table_ref[pl.ds(first_row + a, 1), pl.ds((first_col + q) * BLK, BLK)])
                                    for q in range(per_half)
                                ],
                                axis=1,
                            ).astype(BF16)
                            for a in range(blocks)
                        ],
                        axis=0,
                    )
                    applied = lax.dot_general(
                        tapered, innov, (((1,), (1,)), ((), ())), preferred_element_type=F32
                    )
                    total = applied if total is None else total + applied
                if col > 0:
                    total = total + sum_ref[...]
                elif n_before > 0:
                    total = total + before_refs[row][...]
                sum_ref[...] = total
            if send is not None:
                out_refs[row][...] = sum_ref[...].astype(send).T

    pairs = blocks * blocks * n_row * n_col
    out = (cells, columns) if send is None else (columns, cells)
    return pl.pallas_call(
        kernel,
        out_shape=[jax.ShapeDtypeStruct(out, F32 if send is None else send)] * n_row,
        in_specs=[VMEM] + [VMEM] * (n_stack + n_col + n_before),
        out_specs=[VMEM] * n_row,
        scratch_shapes=[
            pltpu.VMEM((BLK, BLK), F32),
            pltpu.VMEM((cells, members), BF16),
            pltpu.VMEM((cells, columns), F32),
        ],
        compiler_params=pltpu.CompilerParams(vmem_limit_bytes=24 * 2**20),
        cost_estimate=pl.CostEstimate(
            flops=16 * pairs * BLK * BLK * members,
            bytes_accessed=n_col * (members + columns) * cells * 2,
            transcendentals=BLK * BLK,
        ),
        name="increment_rows",
    )(table, *row_stacks, *col_parts, *before)


def stack(parts):
    heights = [part.shape[0] for part in parts]

    def kernel(*refs):
        start = 0
        for ref, height in zip(refs, heights):
            refs[-1][pl.ds(start, height), :] = ref[...]
            start += height

    return pl.pallas_call(
        kernel,
        out_shape=jax.ShapeDtypeStruct((sum(heights), parts[0].shape[1]), parts[0].dtype),
        in_specs=[VMEM] * len(parts),
        out_specs=VMEM,
        compiler_params=SMALL,
        cost_estimate=pl.CostEstimate(flops=1000000000, bytes_accessed=0, transcendentals=0),
        name="stack",
    )(*parts)


def add_up(own, received):
    def kernel(*refs):
        total = refs[0][...]
        for ref in refs[1:-1]:
            total = total + ref[...].astype(F32)
        refs[-1][...] = total

    return pl.pallas_call(
        kernel,
        out_shape=jax.ShapeDtypeStruct(own.shape, F32),
        in_specs=[VMEM] * (1 + len(received)),
        out_specs=VMEM,
        compiler_params=SMALL,
        name="add_up",
    )(own, *received)


def swap(x, axis, size, flip):
    return lax.ppermute(x, axis, [(i, i ^ flip) for i in range(size)])


def solution(mesh):
    n_rows, n_cols = mesh.shape["rows"], mesh.shape["cols"]

    def local(anomalies, innovations, pair_rows, pair_cols, pair_dist, pair_counts):
        per_dev = anomalies.shape[0] // BLK
        members = anomalies.shape[1]
        anom, innov = anomalies.T, innovations.T
        packed = jnp.concatenate([anom, innov], axis=0)
        near = list(range(0, n_rows, 2))
        far = [flip + 1 for flip in near]
        places, held = [(anom, 0)], [anom]
        while len(places) < n_cols:
            outgoing = held[0] if len(held) == 1 else stack(held)
            arrived = swap(outgoing, "cols", n_cols, len(places))
            places += [(arrived, i * members) for i in range(len(places))]
            held.append(arrived)
        near_parts = [packed] + [swap(packed, "rows", n_rows, flip) for flip in near[1:]]
        table = pair_table(
            pair_rows, pair_cols, pair_dist, pair_counts, n_cols * per_dev, n_rows * per_dev, per_dev, members
        )

        far_parts = [swap(part, "rows", n_rows, 1) for part in near_parts]
        others = list(range(1, n_cols))
        early = len(near) // 2
        first = increment_rows(table, places[1:2], [1], members, near_parts[:early], near[:early], [], None)
        before = dict(
            zip(
                others[:1],
                increment_rows(table, places[1:2], [1], members, near_parts[early:], near[early:], first, None),
            )
        )
        before.update(
            zip(others[1:], increment_rows(table, places[2:], others[1:], members, near_parts, near, [], None))
        )
        received = []
        for flip in others:
            (part,) = increment_rows(table, [places[flip]], [flip], members, far_parts, far, [before[flip]], BF16)
            received.append(swap(part, "cols", n_cols, flip))
        (own,) = increment_rows(
            table, [places[0]], [0], members, near_parts + far_parts, near + far, [], F32
        )
        return add_up(own, received).T

    spread = P(("rows", "cols"), None)
    pairs = P("rows", "cols")
    return jax.shard_map(
        local,
        mesh=mesh,
        in_specs=(spread, spread, pairs, pairs, pairs, pairs),
        out_specs=spread,
        check_vma=False,
    )
```

```python
import jax
import jax.numpy as jnp
from jax import lax
from jax.experimental import pallas as pl
from jax.experimental.pallas import tpu as pltpu
from jax.sharding import PartitionSpec as P

BLK = 128
TAPER_CELLS = 8
DIST_SCALE = 4.0
HALF = BLK // 2
SMALL = pltpu.CompilerParams(vmem_limit_bytes=4 * 2**20)

F32 = jnp.float32
BF16 = jnp.bfloat16
VMEM = pl.BlockSpec(memory_space=pltpu.VMEM)
SMEM = pl.BlockSpec(memory_space=pltpu.SMEM)


def pair_table(pair_rows, pair_cols, pair_dist, pair_counts, row_blocks, col_blocks, per_dev, members):
    def kernel(rows_ref, cols_ref, dist_ref, count_ref, table_ref):
        slots = rows_ref.shape[1]
        row_flip = lax.axis_index("cols") * per_dev
        col_flip = lax.axis_index("rows") * per_dev
        live = lax.broadcasted_iota(jnp.int32, (1, slots), 1) < count_ref[0, 0]
        code = jnp.where(live, dist_ref[...] + 1, 0).astype(F32)
        row_place = lax.broadcasted_iota(jnp.int32, (row_blocks, slots), 0)
        col_place = lax.broadcasted_iota(jnp.int32, (col_blocks, slots), 0)
        left = jnp.where(row_place == (rows_ref[...] ^ row_flip), code, 0.0).astype(BF16)
        right = jnp.where(col_place == (cols_ref[...] ^ col_flip), 1.0, 0.0).astype(BF16)
        table = lax.dot_general(left, right, (((1,), (1,)), ((), ())), preferred_element_type=F32)
        spread = lax.broadcasted_iota(jnp.int32, (col_blocks, col_blocks * HALF), 1) // HALF
        spread = (spread == lax.broadcasted_iota(jnp.int32, spread.shape, 0)).astype(F32).astype(BF16)
        wide = jnp.dot(table.astype(BF16), spread, preferred_element_type=F32)
        weight = jnp.exp((1.0 - wide) / DIST_SCALE) * (1.0 / (members - 1))
        table_ref[...] = jnp.where(wide > 0.5, weight, 0.0)

    return pl.pallas_call(
        kernel,
        out_shape=jax.ShapeDtypeStruct((row_blocks, col_blocks * HALF), F32),
        in_specs=[VMEM, VMEM, VMEM, SMEM],
        out_specs=VMEM,
        compiler_params=SMALL,
        name="pair_table",
    )(pair_rows, pair_cols, pair_dist, pair_counts)


def halves_apart(packed):
    height, cells = packed.shape
    wide = cells // 2

    def kernel(in_ref, out_ref):
        source = lax.broadcasted_iota(jnp.int32, (cells, cells), 0)
        lane = lax.broadcasted_iota(jnp.int32, (cells, cells), 1)
        inner = lane % wide
        wanted = inner // HALF * BLK + lane // wide * HALF + inner % HALF
        order = (source == wanted).astype(F32).astype(BF16)
        out_ref[...] = jnp.dot(in_ref[...], order, preferred_element_type=F32).astype(BF16)

    return pl.pallas_call(
        kernel,
        out_shape=jax.ShapeDtypeStruct((height, cells), BF16),
        in_specs=[VMEM],
        out_specs=VMEM,
        compiler_params=SMALL,
        name="halves_apart",
    )(packed)


def fade(shape, axis, rising):
    place = lax.broadcasted_iota(jnp.int32, shape, axis) % HALF
    return jnp.exp((place - HALF if rising else -place).astype(F32) / TAPER_CELLS)


def half_states(col_parts, members):
    columns = col_parts[0].shape[0] - members
    cells = col_parts[0].shape[1]
    wide = cells // 2
    blocks = cells // BLK
    count = len(col_parts)

    def kernel(*refs):
        owner = lax.broadcasted_iota(jnp.int32, (1, wide), 1) // HALF
        for col_ref, out_ref in zip(refs[:count], refs[count:]):
            for half in range(2):
                span = pl.ds(half * wide, wide)
                right = col_ref[pl.ds(0, members), span]
                innov = col_ref[pl.ds(members, columns), span].astype(F32)
                innov = (innov * fade((1, wide), 1, half == 0)).astype(BF16)
                spaced = jnp.concatenate(
                    [right * (owner == q).astype(F32).astype(BF16) for q in range(blocks)], axis=0
                )
                out_ref[pl.ds(half * columns, columns), :] = lax.dot_general(
                    innov, spaced, (((1,), (1,)), ((), ())), preferred_element_type=F32
                )

    return pl.pallas_call(
        kernel,
        out_shape=[jax.ShapeDtypeStruct((2 * columns, blocks * members), F32)] * count,
        in_specs=[VMEM] * count,
        out_specs=[VMEM] * count,
        compiler_params=SMALL,
        name="half_states",
    )(*col_parts)


def increment_rows(table, places, row_flips, members, col_parts, states, col_flips, before, send):
    cells = col_parts[0].shape[1]
    columns = col_parts[0].shape[0] - members
    blocks = cells // BLK
    wide = cells // 2
    lanes = 2 * members
    row_stacks = []
    for stacked, _ in places:
        if all(stacked is not known for known in row_stacks):
            row_stacks.append(stacked)
    spots = [
        ([stacked is known for known in row_stacks].index(True), start) for stacked, start in places
    ]
    n_row, n_stack, n_col, n_before = len(places), len(row_stacks), len(col_parts), len(before)

    def kernel(table_ref, *refs):
        refs = list(refs)
        row_refs, col_refs, state_refs, before_refs, out_refs = (
            [refs.pop(0) for _ in range(n)] for n in (n_stack, n_col, n_col, n_before, n_row)
        )
        tile_ref, fade_ref, left_ref, total_ref, sum_ref = refs
        gap = lax.broadcasted_iota(jnp.int32, (HALF, wide), 0)
        gap = gap - lax.broadcasted_iota(jnp.int32, (HALF, wide), 1) % HALF
        tile_ref[...] = jnp.exp(-jnp.abs(gap).astype(F32) / TAPER_CELLS)
        for half in range(2):
            fade_ref[half] = fade((HALF, columns), 0, half == 0)
        for row in range(n_row):
            left = row_refs[spots[row][0]][pl.ds(spots[row][1], members), :].T
            for a in range(blocks):
                for half in range(2):
                    left_ref[half, pl.ds(a * HALF, HALF), :] = left[a * BLK + half * HALF : a * BLK + (half + 1) * HALF]
            first_row = row_flips[row] * blocks
            for col in range(n_col):
                weights = [
                    tile_ref[...] * table_ref[pl.ds(first_row + a, 1), pl.ds(col_flips[col] * wide, wide)]
                    for a in range(blocks)
                ]
                for half in range(2):
                    span = pl.ds(half * wide, wide)
                    right = col_refs[col][pl.ds(0, members), span]
                    innov = col_refs[col][pl.ds(members, columns), span]
                    products = jnp.dot(left_ref[half], right, preferred_element_type=F32)
                    tapered = jnp.concatenate(
                        [
                            (products[a * HALF : (a + 1) * HALF] * weights[a]).astype(BF16)
                            for a in range(blocks)
                        ],
                        axis=0,
                    )
                    applied = lax.dot_general(
                        tapered, innov, (((1,), (1,)), ((), ())), preferred_element_type=F32
                    )
                    total_ref[half] = applied if col == 0 else total_ref[half] + applied
            dest_ref = sum_ref if send is not None else out_refs[row]
            for a in range(blocks):
                for half in range(2):
                    cross = None
                    for col in range(n_col):
                        for group in range(blocks * members // lanes):
                            start = col_flips[col] * wide + group * lanes
                            term = (
                                state_refs[col][pl.ds((1 - half) * columns, columns), pl.ds(group * lanes, lanes)]
                                * table_ref[pl.ds(first_row + a, 1), pl.ds(start, lanes)]
                            )
                            cross = term if cross is None else cross + term
                    cross = (cross[:, :members] + cross[:, members:]).astype(BF16)
                    far_side = lax.dot_general(
                        left_ref[half, pl.ds(a * HALF, HALF), :],
                        cross,
                        (((1,), (1,)), ((), ())),
                        preferred_element_type=F32,
                    )
                    total = total_ref[half, pl.ds(a * HALF, HALF), :] + far_side * fade_ref[half]
                    cells_here = pl.ds(a * BLK + half * HALF, HALF)
                    if n_before > 0:
                        total = total + before_refs[row][cells_here, :]
                    dest_ref[cells_here, :] = total
            if send is not None:
                out_refs[row][...] = sum_ref[...].astype(send).T

    pairs = blocks * blocks * n_row * n_col
    out = (cells, columns) if send is None else (columns, cells)
    return pl.pallas_call(
        kernel,
        out_shape=[jax.ShapeDtypeStruct(out, F32 if send is None else send)] * n_row,
        in_specs=[VMEM] * (1 + n_stack + 2 * n_col + n_before),
        out_specs=[VMEM] * n_row,
        scratch_shapes=[
            pltpu.VMEM((HALF, wide), F32),
            pltpu.VMEM((2, HALF, columns), F32),
            pltpu.VMEM((2, wide, members), BF16),
            pltpu.VMEM((2, wide, columns), F32),
            pltpu.VMEM((cells, columns), F32),
        ],
        compiler_params=pltpu.CompilerParams(vmem_limit_bytes=24 * 2**20),
        cost_estimate=pl.CostEstimate(
            flops=16 * pairs * BLK * BLK * members,
            bytes_accessed=n_col * (members + columns) * cells * 2,
            transcendentals=BLK * BLK,
        ),
        name="increment_rows",
    )(table, *row_stacks, *col_parts, *states, *before)


def stack(parts):
    heights = [part.shape[0] for part in parts]

    def kernel(*refs):
        start = 0
        for ref, height in zip(refs, heights):
            refs[-1][pl.ds(start, height), :] = ref[...]
            start += height

    return pl.pallas_call(
        kernel,
        out_shape=jax.ShapeDtypeStruct((sum(heights), parts[0].shape[1]), parts[0].dtype),
        in_specs=[VMEM] * len(parts),
        out_specs=VMEM,
        compiler_params=SMALL,
        cost_estimate=pl.CostEstimate(flops=1000000000, bytes_accessed=0, transcendentals=0),
        name="stack",
    )(*parts)


def add_up(own, received):
    def kernel(*refs):
        total = refs[0][...]
        for ref in refs[1:-1]:
            total = total + ref[...].astype(F32)
        refs[-1][...] = total

    return pl.pallas_call(
        kernel,
        out_shape=jax.ShapeDtypeStruct(own.shape, F32),
        in_specs=[VMEM] * (1 + len(received)),
        out_specs=VMEM,
        compiler_params=SMALL,
        name="add_up",
    )(own, *received)


def swap(x, axis, size, flip):
    return lax.ppermute(x, axis, [(i, i ^ flip) for i in range(size)])


def solution(mesh):
    n_rows, n_cols = mesh.shape["rows"], mesh.shape["cols"]

    def local(anomalies, innovations, pair_rows, pair_cols, pair_dist, pair_counts):
        per_dev = anomalies.shape[0] // BLK
        members = anomalies.shape[1]
        anom, innov = anomalies.T, innovations.T
        packed = halves_apart(jnp.concatenate([anom, innov], axis=0))
        near = list(range(0, n_rows, 2))
        far = [flip + 1 for flip in near]
        places, held = [(anom, 0)], [anom]
        while len(places) < n_cols:
            outgoing = held[0] if len(held) == 1 else stack(held)
            arrived = swap(outgoing, "cols", n_cols, len(places))
            places += [(arrived, i * members) for i in range(len(places))]
            held.append(arrived)
        near_parts = [packed] + [swap(packed, "rows", n_rows, flip) for flip in near[1:]]
        table = pair_table(
            pair_rows, pair_cols, pair_dist, pair_counts, n_cols * per_dev, n_rows * per_dev, per_dev, members
        )

        far_parts = [swap(part, "rows", n_rows, 1) for part in near_parts]
        others = list(range(1, n_cols))
        early = len(near) // 2
        near_states = half_states(near_parts[:early], members) + half_states(near_parts[early:], members)
        before = dict(
            zip(
                others[:1],
                increment_rows(table, places[1:2], [1], members, near_parts, near_states, near, [], None),
            )
        )
        before.update(
            zip(
                others[1:],
                increment_rows(table, places[2:], others[1:], members, near_parts, near_states, near, [], None),
            )
        )
        far_states = half_states(far_parts, members)
        received = []
        for flip in others:
            (part,) = increment_rows(
                table, [places[flip]], [flip], members, far_parts, far_states, far, [before[flip]], BF16
            )
            received.append(swap(part, "cols", n_cols, flip))
        (own,) = increment_rows(
            table,
            [places[0]],
            [0],
            members,
            near_parts + far_parts,
            [*near_states, *far_states],
            near + far,
            [],
            F32,
        )
        return add_up(own, received).T

    spread = P(("rows", "cols"), None)
    pairs = P("rows", "cols")
    return jax.shard_map(
        local,
        mesh=mesh,
        in_specs=(spread, spread, pairs, pairs, pairs, pairs),
        out_specs=spread,
        check_vma=False,
    )
```

```python
import jax
import jax.numpy as jnp
from jax import lax
from jax.experimental import pallas as pl
from jax.experimental.pallas import tpu as pltpu
from jax.sharding import PartitionSpec as P

BLK = 128
TAPER_CELLS = 8
DIST_SCALE = 4.0
HALF = BLK // 2
SMALL = pltpu.CompilerParams(vmem_limit_bytes=4 * 2**20)

F32 = jnp.float32
BF16 = jnp.bfloat16
VMEM = pl.BlockSpec(memory_space=pltpu.VMEM)
SMEM = pl.BlockSpec(memory_space=pltpu.SMEM)


def pair_table(pair_rows, pair_cols, pair_dist, pair_counts, row_blocks, col_blocks, per_dev, members):
    def kernel(rows_ref, cols_ref, dist_ref, count_ref, table_ref):
        slots = rows_ref.shape[1]
        row_flip = lax.axis_index("cols") * per_dev
        col_flip = lax.axis_index("rows") * per_dev
        live = lax.broadcasted_iota(jnp.int32, (1, slots), 1) < count_ref[0, 0]
        code = jnp.where(live, dist_ref[...] + 1, 0).astype(F32)
        row_place = lax.broadcasted_iota(jnp.int32, (row_blocks, slots), 0)
        col_place = lax.broadcasted_iota(jnp.int32, (col_blocks, slots), 0)
        left = jnp.where(row_place == (rows_ref[...] ^ row_flip), code, 0.0).astype(BF16)
        right = jnp.where(col_place == (cols_ref[...] ^ col_flip), 1.0, 0.0).astype(BF16)
        table = lax.dot_general(left, right, (((1,), (1,)), ((), ())), preferred_element_type=F32)
        spread = lax.broadcasted_iota(jnp.int32, (col_blocks, col_blocks * HALF), 1) // HALF
        spread = (spread == lax.broadcasted_iota(jnp.int32, spread.shape, 0)).astype(F32).astype(BF16)
        wide = jnp.dot(table.astype(BF16), spread, preferred_element_type=F32)
        weight = jnp.exp((1.0 - wide) / DIST_SCALE) * (1.0 / (members - 1))
        table_ref[...] = jnp.where(wide > 0.5, weight, 0.0)

    return pl.pallas_call(
        kernel,
        out_shape=jax.ShapeDtypeStruct((row_blocks, col_blocks * HALF), F32),
        in_specs=[VMEM, VMEM, VMEM, SMEM],
        out_specs=VMEM,
        compiler_params=SMALL,
        name="pair_table",
    )(pair_rows, pair_cols, pair_dist, pair_counts)


def halves_apart(packed):
    height, cells = packed.shape
    wide = cells // 2

    def kernel(in_ref, out_ref):
        source = lax.broadcasted_iota(jnp.int32, (cells, cells), 0)
        lane = lax.broadcasted_iota(jnp.int32, (cells, cells), 1)
        inner = lane % wide
        wanted = inner // HALF * BLK + lane // wide * HALF + inner % HALF
        order = (source == wanted).astype(F32).astype(BF16)
        out_ref[...] = jnp.dot(in_ref[...], order, preferred_element_type=F32).astype(BF16)

    return pl.pallas_call(
        kernel,
        out_shape=jax.ShapeDtypeStruct((height, cells), BF16),
        in_specs=[VMEM],
        out_specs=VMEM,
        compiler_params=SMALL,
        name="halves_apart",
    )(packed)


def fade(shape, axis, rising):
    place = lax.broadcasted_iota(jnp.int32, shape, axis) % HALF
    return jnp.exp((place - HALF if rising else -place).astype(F32) / TAPER_CELLS)


def fill_states(col_ref, out_ref, members):
    columns = col_ref.shape[0] - members
    wide = col_ref.shape[1] // 2
    owner = lax.broadcasted_iota(jnp.int32, (1, wide), 1) // HALF
    for half in range(2):
        span = pl.ds(half * wide, wide)
        right = col_ref[pl.ds(0, members), span]
        innov = col_ref[pl.ds(members, columns), span].astype(F32)
        innov = (innov * fade((1, wide), 1, half == 0)).astype(BF16)
        spaced = jnp.concatenate(
            [right * (owner == q).astype(F32).astype(BF16) for q in range(wide // HALF)], axis=0
        )
        out_ref[pl.ds(half * columns, columns), :] = lax.dot_general(
            innov, spaced, (((1,), (1,)), ((), ())), preferred_element_type=F32
        )


def increment_rows(table, places, row_flips, members, col_parts, states, col_flips, before, send):
    cells = col_parts[0].shape[1]
    columns = col_parts[0].shape[0] - members
    blocks = cells // BLK
    wide = cells // 2
    lanes = 2 * members
    row_stacks = []
    for stacked, _ in places:
        if all(stacked is not known for known in row_stacks):
            row_stacks.append(stacked)
    spots = [
        ([stacked is known for known in row_stacks].index(True), start) for stacked, start in places
    ]
    n_row, n_stack, n_col, n_before = len(places), len(row_stacks), len(col_parts), len(before)
    fresh = n_col if states is None else 0
    states = [] if states is None else states

    def kernel(table_ref, *refs):
        refs = list(refs)
        row_refs, col_refs, state_refs, before_refs, out_refs, fresh_refs = (
            [refs.pop(0) for _ in range(n)]
            for n in (n_stack, n_col, len(states), n_before, n_row, fresh)
        )
        for col_ref, fresh_ref in zip(col_refs, fresh_refs):
            fill_states(col_ref, fresh_ref, members)
        state_refs = state_refs + fresh_refs
        tile_ref, fade_ref, left_ref, total_ref, sum_ref = refs
        gap = lax.broadcasted_iota(jnp.int32, (HALF, wide), 0)
        gap = gap - lax.broadcasted_iota(jnp.int32, (HALF, wide), 1) % HALF
        tile_ref[...] = jnp.exp(-jnp.abs(gap).astype(F32) / TAPER_CELLS)
        for half in range(2):
            fade_ref[half] = fade((HALF, columns), 0, half == 0)
        for row in range(n_row):
            left = row_refs[spots[row][0]][pl.ds(spots[row][1], members), :].T
            for a in range(blocks):
                for half in range(2):
                    left_ref[half, pl.ds(a * HALF, HALF), :] = left[a * BLK + half * HALF : a * BLK + (half + 1) * HALF]
            first_row = row_flips[row] * blocks
            for col in range(n_col):
                weights = [
                    tile_ref[...] * table_ref[pl.ds(first_row + a, 1), pl.ds(col_flips[col] * wide, wide)]
                    for a in range(blocks)
                ]
                for half in range(2):
                    span = pl.ds(half * wide, wide)
                    right = col_refs[col][pl.ds(0, members), span]
                    innov = col_refs[col][pl.ds(members, columns), span]
                    products = jnp.dot(left_ref[half], right, preferred_element_type=F32)
                    tapered = jnp.concatenate(
                        [
                            (products[a * HALF : (a + 1) * HALF] * weights[a]).astype(BF16)
                            for a in range(blocks)
                        ],
                        axis=0,
                    )
                    applied = lax.dot_general(
                        tapered, innov, (((1,), (1,)), ((), ())), preferred_element_type=F32
                    )
                    total_ref[half] = applied if col == 0 else total_ref[half] + applied
            dest_ref = sum_ref if send is not None else out_refs[row]
            for a in range(blocks):
                for half in range(2):
                    cross = None
                    for col in range(n_col):
                        for group in range(blocks * members // lanes):
                            start = col_flips[col] * wide + group * lanes
                            term = (
                                state_refs[col][pl.ds((1 - half) * columns, columns), pl.ds(group * lanes, lanes)]
                                * table_ref[pl.ds(first_row + a, 1), pl.ds(start, lanes)]
                            )
                            cross = term if cross is None else cross + term
                    cross = (cross[:, :members] + cross[:, members:]).astype(BF16)
                    far_side = lax.dot_general(
                        left_ref[half, pl.ds(a * HALF, HALF), :],
                        cross,
                        (((1,), (1,)), ((), ())),
                        preferred_element_type=F32,
                    )
                    total = total_ref[half, pl.ds(a * HALF, HALF), :] + far_side * fade_ref[half]
                    cells_here = pl.ds(a * BLK + half * HALF, HALF)
                    if n_before > 0:
                        total = total + before_refs[row][cells_here, :]
                    dest_ref[cells_here, :] = total
            if send is not None:
                out_refs[row][...] = sum_ref[...].astype(send).T

    pairs = blocks * blocks * n_row * n_col
    out = (cells, columns) if send is None else (columns, cells)
    return pl.pallas_call(
        kernel,
        out_shape=[jax.ShapeDtypeStruct(out, F32 if send is None else send)] * n_row
        + [jax.ShapeDtypeStruct((2 * columns, blocks * members), F32)] * fresh,
        in_specs=[VMEM] * (1 + n_stack + n_col + len(states) + n_before),
        out_specs=[VMEM] * (n_row + fresh),
        scratch_shapes=[
            pltpu.VMEM((HALF, wide), F32),
            pltpu.VMEM((2, HALF, columns), F32),
            pltpu.VMEM((2, wide, members), BF16),
            pltpu.VMEM((2, wide, columns), F32),
            pltpu.VMEM((cells, columns), F32),
        ],
        compiler_params=pltpu.CompilerParams(vmem_limit_bytes=24 * 2**20),
        cost_estimate=pl.CostEstimate(
            flops=16 * pairs * BLK * BLK * members,
            bytes_accessed=n_col * (members + columns) * cells * 2,
            transcendentals=BLK * BLK,
        ),
        name="increment_rows",
    )(table, *row_stacks, *col_parts, *states, *before)


def stack(parts):
    heights = [part.shape[0] for part in parts]

    def kernel(*refs):
        start = 0
        for ref, height in zip(refs, heights):
            refs[-1][pl.ds(start, height), :] = ref[...]
            start += height

    return pl.pallas_call(
        kernel,
        out_shape=jax.ShapeDtypeStruct((sum(heights), parts[0].shape[1]), parts[0].dtype),
        in_specs=[VMEM] * len(parts),
        out_specs=VMEM,
        compiler_params=SMALL,
        cost_estimate=pl.CostEstimate(flops=1000000000, bytes_accessed=0, transcendentals=0),
        name="stack",
    )(*parts)


def add_up(own, received):
    def kernel(*refs):
        total = refs[0][...]
        for ref in refs[1:-1]:
            total = total + ref[...].astype(F32)
        refs[-1][...] = total

    return pl.pallas_call(
        kernel,
        out_shape=jax.ShapeDtypeStruct(own.shape, F32),
        in_specs=[VMEM] * (1 + len(received)),
        out_specs=VMEM,
        compiler_params=SMALL,
        name="add_up",
    )(own, *received)


def swap(x, axis, size, flip):
    return lax.ppermute(x, axis, [(i, i ^ flip) for i in range(size)])


def solution(mesh):
    n_rows, n_cols = mesh.shape["rows"], mesh.shape["cols"]

    def local(anomalies, innovations, pair_rows, pair_cols, pair_dist, pair_counts):
        per_dev = anomalies.shape[0] // BLK
        members = anomalies.shape[1]
        anom, innov = anomalies.T, innovations.T
        packed = halves_apart(jnp.concatenate([anom, innov], axis=0))
        near = list(range(0, n_rows, 2))
        far = [flip + 1 for flip in near]
        places, held = [(anom, 0)], [anom]
        while len(places) < n_cols:
            outgoing = held[0] if len(held) == 1 else stack(held)
            arrived = swap(outgoing, "cols", n_cols, len(places))
            places += [(arrived, i * members) for i in range(len(places))]
            held.append(arrived)
        near_parts = [packed] + [swap(packed, "rows", n_rows, flip) for flip in near[1:]]
        table = pair_table(
            pair_rows, pair_cols, pair_dist, pair_counts, n_cols * per_dev, n_rows * per_dev, per_dev, members
        )
        far_parts = [swap(part, "rows", n_rows, 1) for part in near_parts]
        others = list(range(1, n_cols))
        first, *near_states = increment_rows(table, places[1:2], [1], members, near_parts, None, near, [], None)
        before = {1: first}
        before.update(
            zip(
                others[1:],
                increment_rows(table, places[2:], others[1:], members, near_parts, near_states, near, [], None),
            )
        )
        received, far_states = [], None
        for flip in range(n_cols - 1, 0, -1):
            part, *fresh = increment_rows(
                table, [places[flip]], [flip], members, far_parts, far_states, far, [before[flip]], BF16
            )
            far_states = far_states or fresh
            if flip > 1:
                before[flip - 1], _ = lax.optimization_barrier((before[flip - 1], part))
            received.append(swap(part, "cols", n_cols, flip))
        (own,) = increment_rows(
            table,
            [places[0]],
            [0],
            members,
            near_parts + far_parts,
            [*near_states, *far_states],
            near + far,
            [],
            F32,
        )
        return add_up(own, received).T

    spread = P(("rows", "cols"), None)
    pairs = P("rows", "cols")
    return jax.shard_map(
        local,
        mesh=mesh,
        in_specs=(spread, spread, pairs, pairs, pairs, pairs),
        out_specs=spread,
        check_vma=False,
    )
```

```python
import jax
import jax.numpy as jnp
from jax import lax
from jax.experimental import pallas as pl
from jax.experimental.pallas import tpu as pltpu
from jax.sharding import PartitionSpec as P

BLK = 128
TAPER_CELLS = 8
DIST_SCALE = 4.0
HALF = BLK // 2
SMALL = pltpu.CompilerParams(vmem_limit_bytes=4 * 2**20)

F32 = jnp.float32
BF16 = jnp.bfloat16
VMEM = pl.BlockSpec(memory_space=pltpu.VMEM)
SMEM = pl.BlockSpec(memory_space=pltpu.SMEM)


def pair_table(pair_rows, pair_cols, pair_dist, pair_counts, row_blocks, col_blocks, per_dev, members):
    def kernel(rows_ref, cols_ref, dist_ref, count_ref, table_ref):
        slots = rows_ref.shape[1]
        row_flip = lax.axis_index("cols") * per_dev
        col_flip = lax.axis_index("rows") * per_dev
        live = lax.broadcasted_iota(jnp.int32, (1, slots), 1) < count_ref[0, 0]
        code = jnp.where(live, dist_ref[...] + 1, 0).astype(F32)
        row_place = lax.broadcasted_iota(jnp.int32, (row_blocks, slots), 0)
        col_place = lax.broadcasted_iota(jnp.int32, (col_blocks, slots), 0)
        left = jnp.where(row_place == (rows_ref[...] ^ row_flip), code, 0.0).astype(BF16)
        right = jnp.where(col_place == (cols_ref[...] ^ col_flip), 1.0, 0.0).astype(BF16)
        table = lax.dot_general(left, right, (((1,), (1,)), ((), ())), preferred_element_type=F32)
        spread = lax.broadcasted_iota(jnp.int32, (col_blocks, col_blocks * HALF), 1) // HALF
        spread = (spread == lax.broadcasted_iota(jnp.int32, spread.shape, 0)).astype(F32).astype(BF16)
        wide = jnp.dot(table.astype(BF16), spread, preferred_element_type=F32)
        weight = jnp.exp((1.0 - wide) / DIST_SCALE) * (1.0 / (members - 1))
        table_ref[...] = jnp.where(wide > 0.5, weight, 0.0)

    return pl.pallas_call(
        kernel,
        out_shape=jax.ShapeDtypeStruct((row_blocks, col_blocks * HALF), F32),
        in_specs=[VMEM, VMEM, VMEM, SMEM],
        out_specs=VMEM,
        compiler_params=SMALL,
        name="pair_table",
    )(pair_rows, pair_cols, pair_dist, pair_counts)


def halves_apart(packed):
    height, cells = packed.shape
    wide = cells // 2

    def kernel(in_ref, out_ref):
        source = lax.broadcasted_iota(jnp.int32, (cells, cells), 0)
        lane = lax.broadcasted_iota(jnp.int32, (cells, cells), 1)
        inner = lane % wide
        wanted = inner // HALF * BLK + lane // wide * HALF + inner % HALF
        order = (source == wanted).astype(F32).astype(BF16)
        out_ref[...] = jnp.dot(in_ref[...], order, preferred_element_type=F32).astype(BF16)

    return pl.pallas_call(
        kernel,
        out_shape=jax.ShapeDtypeStruct((height, cells), BF16),
        in_specs=[VMEM],
        out_specs=VMEM,
        compiler_params=SMALL,
        name="halves_apart",
    )(packed)


def fade(shape, axis, rising):
    place = lax.broadcasted_iota(jnp.int32, shape, axis) % HALF
    return jnp.exp((place - HALF if rising else -place).astype(F32) / TAPER_CELLS)


def fill_states(col_ref, out_ref, members):
    columns = col_ref.shape[0] - members
    wide = col_ref.shape[1] // 2
    owner = lax.broadcasted_iota(jnp.int32, (1, wide), 1) // HALF
    for half in range(2):
        span = pl.ds(half * wide, wide)
        right = col_ref[pl.ds(0, members), span]
        innov = col_ref[pl.ds(members, columns), span].astype(F32)
        innov = (innov * fade((1, wide), 1, half == 0)).astype(BF16)
        spaced = jnp.concatenate(
            [right * (owner == q).astype(F32).astype(BF16) for q in range(wide // HALF)], axis=0
        )
        out_ref[pl.ds(half * columns, columns), :] = lax.dot_general(
            innov, spaced, (((1,), (1,)), ((), ())), preferred_element_type=F32
        )


def increment_rows(table, places, row_flips, members, col_parts, states, col_flips, before, send, lefts=None):
    cells = col_parts[0].shape[1]
    columns = col_parts[0].shape[0] - members
    blocks = cells // BLK
    wide = cells // 2
    lanes = 2 * members
    row_stacks = []
    for stacked, _ in places:
        if all(stacked is not known for known in row_stacks):
            row_stacks.append(stacked)
    spots = [
        ([stacked is known for known in row_stacks].index(True), start) for stacked, start in places
    ]
    n_row, n_stack, n_col, n_before = len(places), len(row_stacks), len(col_parts), len(before)
    fresh = n_col if states is None else 0
    states = [] if states is None else states
    lefts = [] if lefts is None else lefts
    handed = n_row if n_before == 0 and send is None else 0
    if lefts:
        row_stacks, n_stack = [], 0

    def kernel(table_ref, *refs):
        refs = list(refs)
        row_refs, col_refs, state_refs, before_refs, known_refs, out_refs, handed_refs, fresh_refs = (
            [refs.pop(0) for _ in range(n)]
            for n in (n_stack, n_col, len(states), n_before, len(lefts), n_row, handed, fresh)
        )
        for col_ref, fresh_ref in zip(col_refs, fresh_refs):
            fill_states(col_ref, fresh_ref, members)
        state_refs = state_refs + fresh_refs
        tile_ref, fade_ref, own_left_ref, total_ref, sum_ref = refs
        gap = lax.broadcasted_iota(jnp.int32, (HALF, wide), 0)
        gap = gap - lax.broadcasted_iota(jnp.int32, (HALF, wide), 1) % HALF
        tile_ref[...] = jnp.exp(-jnp.abs(gap).astype(F32) / TAPER_CELLS)
        for half in range(2):
            fade_ref[half] = fade((HALF, columns), 0, half == 0)
        for row in range(n_row):
            if lefts:
                left_ref = known_refs[row]
            else:
                left_ref = handed_refs[row] if handed else own_left_ref
                left = row_refs[spots[row][0]][pl.ds(spots[row][1], members), :].T
                for a in range(blocks):
                    for half in range(2):
                        start = a * BLK + half * HALF
                        left_ref[half, pl.ds(a * HALF, HALF), :] = left[start : start + HALF]
            first_row = row_flips[row] * blocks
            for col in range(n_col):
                weights = [
                    tile_ref[...] * table_ref[pl.ds(first_row + a, 1), pl.ds(col_flips[col] * wide, wide)]
                    for a in range(blocks)
                ]
                for half in range(2):
                    span = pl.ds(half * wide, wide)
                    right = col_refs[col][pl.ds(0, members), span]
                    innov = col_refs[col][pl.ds(members, columns), span]
                    products = jnp.dot(left_ref[half], right, preferred_element_type=F32)
                    tapered = jnp.concatenate(
                        [
                            (products[a * HALF : (a + 1) * HALF] * weights[a]).astype(BF16)
                            for a in range(blocks)
                        ],
                        axis=0,
                    )
                    applied = lax.dot_general(
                        tapered, innov, (((1,), (1,)), ((), ())), preferred_element_type=F32
                    )
                    total_ref[half] = applied if col == 0 else total_ref[half] + applied
            dest_ref = sum_ref if send is not None else out_refs[row]
            for a in range(blocks):
                for half in range(2):
                    cross = None
                    for col in range(n_col):
                        for group in range(blocks * members // lanes):
                            start = col_flips[col] * wide + group * lanes
                            term = (
                                state_refs[col][pl.ds((1 - half) * columns, columns), pl.ds(group * lanes, lanes)]
                                * table_ref[pl.ds(first_row + a, 1), pl.ds(start, lanes)]
                            )
                            cross = term if cross is None else cross + term
                    cross = (cross[:, :members] + cross[:, members:]).astype(BF16)
                    far_side = lax.dot_general(
                        left_ref[half, pl.ds(a * HALF, HALF), :],
                        cross,
                        (((1,), (1,)), ((), ())),
                        preferred_element_type=F32,
                    )
                    total = total_ref[half, pl.ds(a * HALF, HALF), :] + far_side * fade_ref[half]
                    cells_here = pl.ds(a * BLK + half * HALF, HALF)
                    if n_before > 0:
                        total = total + before_refs[row][cells_here, :]
                    dest_ref[cells_here, :] = total
            if send is not None:
                out_refs[row][...] = sum_ref[...].astype(send).T

    pairs = blocks * blocks * n_row * n_col
    out = (cells, columns) if send is None else (columns, cells)
    return pl.pallas_call(
        kernel,
        out_shape=[jax.ShapeDtypeStruct(out, F32 if send is None else send)] * n_row
        + [jax.ShapeDtypeStruct((2, wide, members), BF16)] * handed
        + [jax.ShapeDtypeStruct((2 * columns, blocks * members), F32)] * fresh,
        in_specs=[VMEM] * (1 + n_stack + n_col + len(states) + n_before + len(lefts)),
        out_specs=[VMEM] * (n_row + handed + fresh),
        scratch_shapes=[
            pltpu.VMEM((HALF, wide), F32),
            pltpu.VMEM((2, HALF, columns), F32),
            pltpu.VMEM((2, wide, members), BF16),
            pltpu.VMEM((2, wide, columns), F32),
            pltpu.VMEM((cells, columns), F32),
        ],
        compiler_params=pltpu.CompilerParams(vmem_limit_bytes=24 * 2**20),
        cost_estimate=pl.CostEstimate(
            flops=16 * pairs * BLK * BLK * members,
            bytes_accessed=n_col * (members + columns) * cells * 2,
            transcendentals=BLK * BLK,
        ),
        name="increment_rows",
    )(table, *row_stacks, *col_parts, *states, *before, *lefts)


def stack(parts):
    heights = [part.shape[0] for part in parts]

    def kernel(*refs):
        start = 0
        for ref, height in zip(refs, heights):
            refs[-1][pl.ds(start, height), :] = ref[...]
            start += height

    return pl.pallas_call(
        kernel,
        out_shape=jax.ShapeDtypeStruct((sum(heights), parts[0].shape[1]), parts[0].dtype),
        in_specs=[VMEM] * len(parts),
        out_specs=VMEM,
        compiler_params=SMALL,
        cost_estimate=pl.CostEstimate(flops=1000000000, bytes_accessed=0, transcendentals=0),
        name="stack",
    )(*parts)


def add_up(own, received):
    def kernel(*refs):
        total = refs[0][...]
        for ref in refs[1:-1]:
            total = total + ref[...].astype(F32)
        refs[-1][...] = total

    return pl.pallas_call(
        kernel,
        out_shape=jax.ShapeDtypeStruct(own.shape, F32),
        in_specs=[VMEM] * (1 + len(received)),
        out_specs=VMEM,
        compiler_params=SMALL,
        name="add_up",
    )(own, *received)


def swap(x, axis, size, flip):
    return lax.ppermute(x, axis, [(i, i ^ flip) for i in range(size)])


def solution(mesh):
    n_rows, n_cols = mesh.shape["rows"], mesh.shape["cols"]

    def local(anomalies, innovations, pair_rows, pair_cols, pair_dist, pair_counts):
        per_dev = anomalies.shape[0] // BLK
        members = anomalies.shape[1]
        anom, innov = anomalies.T, innovations.T
        packed = halves_apart(jnp.concatenate([anom, innov], axis=0))
        near = list(range(0, n_rows, 2))
        far = [flip + 1 for flip in near]
        places, held = [(anom, 0)], [anom]
        while len(places) < n_cols:
            outgoing = held[0] if len(held) == 1 else stack(held)
            arrived = swap(outgoing, "cols", n_cols, len(places))
            places += [(arrived, i * members) for i in range(len(places))]
            held.append(arrived)
        near_parts = [packed] + [swap(packed, "rows", n_rows, flip) for flip in near[1:]]
        table = pair_table(
            pair_rows, pair_cols, pair_dist, pair_counts, n_cols * per_dev, n_rows * per_dev, per_dev, members
        )
        far_parts = [swap(part, "rows", n_rows, 1) for part in near_parts]
        others = list(range(1, n_cols))
        first, left, *near_states = increment_rows(
            table, places[1:2], [1], members, near_parts, None, near, [], None
        )
        rest = increment_rows(table, places[2:], others[1:], members, near_parts, near_states, near, [], None)
        before = dict(zip(others, [first, *rest[: len(others) - 1]]))
        lefts = dict(zip(others, [left, *rest[len(others) - 1 :]]))
        received, far_states = [], None
        for flip in range(n_cols - 1, 0, -1):
            part, *fresh = increment_rows(
                table,
                [places[flip]],
                [flip],
                members,
                far_parts,
                far_states,
                far,
                [before[flip]],
                BF16,
                [lefts[flip]],
            )
            far_states = far_states or fresh
            if flip > 1:
                before[flip - 1], _ = lax.optimization_barrier((before[flip - 1], part))
            received.append(swap(part, "cols", n_cols, flip))
        (own,) = increment_rows(
            table,
            [places[0]],
            [0],
            members,
            near_parts + far_parts,
            [*near_states, *far_states],
            near + far,
            [],
            F32,
        )
        return add_up(own, received).T

    spread = P(("rows", "cols"), None)
    pairs = P("rows", "cols")
    return jax.shard_map(
        local,
        mesh=mesh,
        in_specs=(spread, spread, pairs, pairs, pairs, pairs),
        out_specs=spread,
        check_vma=False,
    )
```

```python
import jax
import jax.numpy as jnp
from jax import lax
from jax.experimental import pallas as pl
from jax.experimental.pallas import tpu as pltpu
from jax.sharding import PartitionSpec as P

BLK = 128
TAPER_CELLS = 8
DIST_SCALE = 4.0
HALF = BLK // 2
SMALL = pltpu.CompilerParams(vmem_limit_bytes=4 * 2**20)

F32 = jnp.float32
BF16 = jnp.bfloat16
VMEM = pl.BlockSpec(memory_space=pltpu.VMEM)
SMEM = pl.BlockSpec(memory_space=pltpu.SMEM)


def pair_table(pair_rows, pair_cols, pair_dist, pair_counts, row_blocks, col_blocks, per_dev, members):
    def kernel(rows_ref, cols_ref, dist_ref, count_ref, table_ref):
        slots = rows_ref.shape[1]
        row_flip = lax.axis_index("cols") * per_dev
        col_flip = lax.axis_index("rows") * per_dev
        live = lax.broadcasted_iota(jnp.int32, (1, slots), 1) < count_ref[0, 0]
        code = jnp.where(live, dist_ref[...] + 1, 0).astype(F32)
        row_place = lax.broadcasted_iota(jnp.int32, (row_blocks, slots), 0)
        col_place = lax.broadcasted_iota(jnp.int32, (col_blocks, slots), 0)
        left = jnp.where(row_place == (rows_ref[...] ^ row_flip), code, 0.0).astype(BF16)
        right = jnp.where(col_place == (cols_ref[...] ^ col_flip), 1.0, 0.0).astype(BF16)
        table = lax.dot_general(left, right, (((1,), (1,)), ((), ())), preferred_element_type=F32)
        spread = lax.broadcasted_iota(jnp.int32, (col_blocks, col_blocks * HALF), 1) // HALF
        spread = (spread == lax.broadcasted_iota(jnp.int32, spread.shape, 0)).astype(F32).astype(BF16)
        wide = jnp.dot(table.astype(BF16), spread, preferred_element_type=F32)
        weight = jnp.exp((1.0 - wide) / DIST_SCALE) * (1.0 / (members - 1))
        table_ref[...] = jnp.where(wide > 0.5, weight, 0.0)

    return pl.pallas_call(
        kernel,
        out_shape=jax.ShapeDtypeStruct((row_blocks, col_blocks * HALF), F32),
        in_specs=[VMEM, VMEM, VMEM, SMEM],
        out_specs=VMEM,
        compiler_params=SMALL,
        name="pair_table",
    )(pair_rows, pair_cols, pair_dist, pair_counts)


def fade(shape, axis, rising):
    place = lax.broadcasted_iota(jnp.int32, shape, axis) % HALF
    return jnp.exp((place - HALF if rising else -place).astype(F32) / TAPER_CELLS)


def fill_states(col_ref, out_ref, members):
    columns = col_ref.shape[0] - members
    wide = col_ref.shape[1] // 2
    owner = lax.broadcasted_iota(jnp.int32, (1, wide), 1) // HALF
    for half in range(2):
        span = pl.ds(half * wide, wide)
        right = col_ref[pl.ds(0, members), span]
        innov = col_ref[pl.ds(members, columns), span].astype(F32)
        innov = (innov * fade((1, wide), 1, half == 0)).astype(BF16)
        spaced = jnp.concatenate(
            [right * (owner == q).astype(F32).astype(BF16) for q in range(wide // HALF)], axis=0
        )
        out_ref[pl.ds(half * columns, columns), :] = lax.dot_general(
            innov, spaced, (((1,), (1,)), ((), ())), preferred_element_type=F32
        )


def increment_rows(table, places, row_flips, members, col_parts, states, col_flips, before, send):
    cells = col_parts[0].shape[1]
    columns = col_parts[0].shape[0] - members
    blocks = cells // BLK
    wide = cells // 2
    lanes = 2 * members
    row_stacks = []
    for stacked, _ in places:
        if all(stacked is not known for known in row_stacks):
            row_stacks.append(stacked)
    spots = [
        ([stacked is known for known in row_stacks].index(True), start) for stacked, start in places
    ]
    n_row, n_stack, n_col, n_before = len(places), len(row_stacks), len(col_parts), len(before)
    fresh = n_col if states is None else 0
    states = [] if states is None else states

    def kernel(table_ref, *refs):
        refs = list(refs)
        row_refs, col_refs, state_refs, before_refs, out_refs, fresh_refs = (
            [refs.pop(0) for _ in range(n)]
            for n in (n_stack, n_col, len(states), n_before, n_row, fresh)
        )
        for col_ref, fresh_ref in zip(col_refs, fresh_refs):
            fill_states(col_ref, fresh_ref, members)
        state_refs = state_refs + fresh_refs
        tile_ref, fade_ref, left_ref, total_ref, sum_ref = refs
        gap = lax.broadcasted_iota(jnp.int32, (HALF, wide), 0)
        gap = gap - lax.broadcasted_iota(jnp.int32, (HALF, wide), 1) % HALF
        tile_ref[...] = jnp.exp(-jnp.abs(gap).astype(F32) / TAPER_CELLS)
        for half in range(2):
            fade_ref[half] = fade((HALF, columns), 0, half == 0)
        for row in range(n_row):
            left = row_refs[spots[row][0]][pl.ds(spots[row][1], members), :].T
            for a in range(blocks):
                for half in range(2):
                    left_ref[half, pl.ds(a * HALF, HALF), :] = left[a * BLK + half * HALF : a * BLK + (half + 1) * HALF]
            first_row = row_flips[row] * blocks
            for col in range(n_col):
                weights = [
                    tile_ref[...] * table_ref[pl.ds(first_row + a, 1), pl.ds(col_flips[col] * wide, wide)]
                    for a in range(blocks)
                ]
                for half in range(2):
                    span = pl.ds(half * wide, wide)
                    right = col_refs[col][pl.ds(0, members), span]
                    innov = col_refs[col][pl.ds(members, columns), span]
                    products = jnp.dot(left_ref[half], right, preferred_element_type=F32)
                    tapered = jnp.concatenate(
                        [
                            (products[a * HALF : (a + 1) * HALF] * weights[a]).astype(BF16)
                            for a in range(blocks)
                        ],
                        axis=0,
                    )
                    applied = lax.dot_general(
                        tapered, innov, (((1,), (1,)), ((), ())), preferred_element_type=F32
                    )
                    total_ref[half] = applied if col == 0 else total_ref[half] + applied
            dest_ref = sum_ref if send is not None else out_refs[row]
            for a in range(blocks):
                for half in range(2):
                    cross = None
                    for col in range(n_col):
                        for group in range(blocks * members // lanes):
                            start = col_flips[col] * wide + group * lanes
                            term = (
                                state_refs[col][pl.ds((1 - half) * columns, columns), pl.ds(group * lanes, lanes)]
                                * table_ref[pl.ds(first_row + a, 1), pl.ds(start, lanes)]
                            )
                            cross = term if cross is None else cross + term
                    cross = (cross[:, :members] + cross[:, members:]).astype(BF16)
                    far_side = lax.dot_general(
                        left_ref[half, pl.ds(a * HALF, HALF), :],
                        cross,
                        (((1,), (1,)), ((), ())),
                        preferred_element_type=F32,
                    )
                    total = total_ref[half, pl.ds(a * HALF, HALF), :] + far_side * fade_ref[half]
                    cells_here = pl.ds(a * BLK + half * HALF, HALF)
                    if n_before > 0:
                        total = total + before_refs[row][cells_here, :]
                    dest_ref[cells_here, :] = total
            if send is not None:
                out_refs[row][...] = sum_ref[...].astype(send).T

    pairs = blocks * blocks * n_row * n_col
    out = (cells, columns) if send is None else (columns, cells)
    return pl.pallas_call(
        kernel,
        out_shape=[jax.ShapeDtypeStruct(out, F32 if send is None else send)] * n_row
        + [jax.ShapeDtypeStruct((2 * columns, blocks * members), F32)] * fresh,
        in_specs=[VMEM] * (1 + n_stack + n_col + len(states) + n_before),
        out_specs=[VMEM] * (n_row + fresh),
        scratch_shapes=[
            pltpu.VMEM((HALF, wide), F32),
            pltpu.VMEM((2, HALF, columns), F32),
            pltpu.VMEM((2, wide, members), BF16),
            pltpu.VMEM((2, wide, columns), F32),
            pltpu.VMEM((cells, columns), F32),
        ],
        compiler_params=pltpu.CompilerParams(vmem_limit_bytes=24 * 2**20),
        cost_estimate=pl.CostEstimate(
            flops=16 * pairs * BLK * BLK * members,
            bytes_accessed=n_col * (members + columns) * cells * 2,
            transcendentals=BLK * BLK,
        ),
        name="increment_rows",
    )(table, *row_stacks, *col_parts, *states, *before)


def stack(parts):
    heights = [part.shape[0] for part in parts]

    def kernel(*refs):
        start = 0
        for ref, height in zip(refs, heights):
            refs[-1][pl.ds(start, height), :] = ref[...]
            start += height

    return pl.pallas_call(
        kernel,
        out_shape=jax.ShapeDtypeStruct((sum(heights), parts[0].shape[1]), parts[0].dtype),
        in_specs=[VMEM] * len(parts),
        out_specs=VMEM,
        compiler_params=SMALL,
        cost_estimate=pl.CostEstimate(flops=1000000000, bytes_accessed=0, transcendentals=0),
        name="stack",
    )(*parts)


def add_up(own, received):
    def kernel(*refs):
        total = refs[0][...]
        for ref in refs[1:-1]:
            total = total + ref[...].astype(F32)
        refs[-1][...] = total

    return pl.pallas_call(
        kernel,
        out_shape=jax.ShapeDtypeStruct(own.shape, F32),
        in_specs=[VMEM] * (1 + len(received)),
        out_specs=VMEM,
        compiler_params=SMALL,
        name="add_up",
    )(own, *received)


def swap(x, axis, size, flip):
    return lax.ppermute(x, axis, [(i, i ^ flip) for i in range(size)])


def solution(mesh):
    n_rows, n_cols = mesh.shape["rows"], mesh.shape["cols"]

    def local(anomalies, innovations, pair_rows, pair_cols, pair_dist, pair_counts):
        per_dev = anomalies.shape[0] // BLK
        members = anomalies.shape[1]
        anom, innov = anomalies.T, innovations.T
        both = jnp.concatenate([anom, innov], axis=0).reshape(-1, per_dev, 2, HALF)
        packed = both.transpose(0, 2, 1, 3).reshape(both.shape[0], -1)
        near = list(range(0, n_rows, 2))
        far = [flip + 1 for flip in near]
        places, held = [(anom, 0)], [anom]
        while len(places) < n_cols:
            outgoing = held[0] if len(held) == 1 else stack(held)
            arrived = swap(outgoing, "cols", n_cols, len(places))
            places += [(arrived, i * members) for i in range(len(places))]
            held.append(arrived)
        near_parts = [packed] + [swap(packed, "rows", n_rows, flip) for flip in near[1:]]
        table = pair_table(
            pair_rows, pair_cols, pair_dist, pair_counts, n_cols * per_dev, n_rows * per_dev, per_dev, members
        )
        far_parts = [swap(part, "rows", n_rows, 1) for part in near_parts]
        others = list(range(1, n_cols))
        first, *near_states = increment_rows(table, places[1:2], [1], members, near_parts, None, near, [], None)
        before = {1: first}
        before.update(
            zip(
                others[1:],
                increment_rows(table, places[2:], others[1:], members, near_parts, near_states, near, [], None),
            )
        )
        received, far_states = [], None
        for flip in range(n_cols - 1, 0, -1):
            part, *fresh = increment_rows(
                table, [places[flip]], [flip], members, far_parts, far_states, far, [before[flip]], BF16
            )
            far_states = far_states or fresh
            if flip > 1:
                before[flip - 1], _ = lax.optimization_barrier((before[flip - 1], part))
            received.append(swap(part, "cols", n_cols, flip))
        (own,) = increment_rows(
            table,
            [places[0]],
            [0],
            members,
            near_parts + far_parts,
            [*near_states, *far_states],
            near + far,
            [],
            F32,
        )
        return add_up(own, received).T

    spread = P(("rows", "cols"), None)
    pairs = P("rows", "cols")
    return jax.shard_map(
        local,
        mesh=mesh,
        in_specs=(spread, spread, pairs, pairs, pairs, pairs),
        out_specs=spread,
        check_vma=False,
    )
```
